32 devices in a mesh: prow: 8 (over z, x), pcol: 4 (over y, core).
Axes of the slice: x: 2, y: 2, z: 4, core: 2. Of those that a mesh axis runs over, the one named last changes fastest.
Arguments:
- pool_inverse: float32 [2048, 2048], P('prow', 'pcol'), may hold values from -6 to 6
- panel_blocks: float32 [1, 2048, 512], P(None, 'prow'), may hold values from -0.1875 to 0.1875
- prev_panel: float32 [1, 512, 512], P(None, 'prow'), may hold values from -0.25 to 0.25
- pivot_inverse: float32 [1, 512, 512], P(None, 'pcol'), may hold values from -6 to 6
- top_column: float32 [512, 2048], P('pcol', 'prow'), may hold values from -6 to 6
- top_diag: float32 [512, 512], P('pcol'), may hold values from -6 to 6
- slot_blocks: int32 [1, 16], replicated, may hold values from -1 to 15, as said below
Outputs:
- column_out: float32 [1, 512, 2048], P(None, 'pcol', 'prow')
- cross_out: float32 [1, 512, 512], P(None, 'pcol')
- diag_out: float32 [1, 512, 512], P(None, 'pcol')
The draws below stay inside these ranges and needn't reach their ends.
Inputs may be any that keep to these rules, and one draw needn't show every extreme that they name: `slot_blocks`: row owner r's slots, entries r * 2 to r * 2 + 1 of a supernode's list, name distinct pool blocks of r * 2 to r * 2 + 1 in ascending order, followed by -1 for unused slots. In every supernode the 2 row owners of some aligned group of 2 use all their slots.
All inputs are finite; a program needn't handle non-finite values.
Results may differ from the reference program's by a relative error of at most 0.0001.
Values sent between devices are 32-bit elements; how exact they have to be, the bound alone decides.
A program may use at most 64 MiB of HBM per device.

```python
import jax
import jax.numpy as jnp
from jax import lax

W = 512
BLK = 128
SLOTS = 2
SN = 1
RBLK = 2
QGRP = 2
NA = 16
M = 2048
PANEL = 2048
N_PROW = 8


def draw_slot_blocks(key, part):
    key_count, key_group, key_order = jax.random.split(jax.random.fold_in(key, 17), 3)
    owners = jnp.arange(N_PROW, dtype=jnp.int32)
    supernodes = jnp.arange(SN, dtype=jnp.int32)
    counts = jax.random.randint(key_count, (SN, N_PROW), 0, SLOTS + 1)
    group_start = jax.random.randint(key_group, (SN, 1), 0, N_PROW // QGRP) * QGRP
    whole_group = (owners[None, :] >= group_start) & (owners[None, :] < group_start + QGRP)
    short_owner = (owners[None, :] == (group_start + QGRP) % N_PROW) & (supernodes[:, None] >= 1)
    top_owner = (owners[None, :] == N_PROW - 1) & (supernodes[:, None] == 0)
    counts = jnp.where(whole_group | top_owner, SLOTS, counts)
    counts = jnp.where(short_owner, SLOTS - 1, counts)
    scores = jax.random.randint(key_order, (SN, N_PROW, RBLK), 0, 1 << 20) * RBLK + jnp.arange(RBLK, dtype=jnp.int32)
    lifted = top_owner[:, :, None] & (jnp.arange(RBLK) == RBLK - 1)[None, None, :]
    scores = jnp.where(lifted, -1, scores)
    chosen = jnp.sort(jnp.argsort(scores, axis=2)[:, :, :SLOTS], axis=2).astype(jnp.int32)
    blocks_global = owners[None, :, None] * RBLK + chosen
    slot_ids = jnp.where(jnp.arange(SLOTS)[None, None, :] < counts[:, :, None], blocks_global, -1)
    return slot_ids.reshape(SN, N_PROW * SLOTS).astype(jnp.int32)


def levels(key, extent, cuts, least, top_value):
    loudness = 1.0
    for dim, shards_of in cuts:
        steps = jax.random.uniform(jax.random.fold_in(jax.random.fold_in(key, 6), dim), (shards_of,), jnp.float32, least / len(cuts), top_value / len(cuts))
        loudness = loudness * jnp.repeat(jnp.exp(steps), extent[dim] // shards_of).reshape((-1,) + (1,) * (len(extent) - 1 - dim))
    return loudness


def centred(own_key, dims, scale, most, cuts=(), held_as=jnp.bfloat16):
    loudness = levels(own_key, dims, cuts, -0.22, 0.18) if cuts else 1.0
    result = jax.random.normal(own_key, dims, jnp.float32) * scale * loudness
    return jnp.minimum(jnp.maximum(result, -most), most).astype(held_as)


def setup_inputs(seed: int = 0) -> dict:
    splits = jax.random.split(jax.random.key(seed), 8)
    return {
        "pool_inverse": centred(splits[0], (M, M), 1.0, 6.0, ((0, 8), (1, 4)), jnp.float32),
        "panel_blocks": centred(splits[1], (SN, PANEL, W), (N_PROW * BLK) ** -0.5, 0.1875, ((1, 8),), jnp.float32),
        "prev_panel": centred(splits[2], (SN, W, W), W ** -0.5, 0.25, ((1, 8),), jnp.float32),
        "pivot_inverse": centred(splits[3], (SN, W, W), 1.0, 6.0, ((1, 4),), jnp.float32),
        "top_column": centred(splits[4], (W, M), 1.0, 6.0, ((0, 4), (1, 8)), jnp.float32),
        "top_diag": centred(splits[5], (W, W), 1.0, 6.0, ((0, 4),), jnp.float32),
        "slot_blocks": draw_slot_blocks(jax.random.fold_in(splits[7], 71), 0),
    }


highest = lax.Precision.HIGHEST


def matmul(left, right):
    return jnp.dot(left, right, precision=highest, preferred_element_type=jnp.float32)


def reference(pool_inverse, panel_blocks, prev_panel, pivot_inverse, top_column, top_diag, slot_blocks):
    chain_column = top_column
    chain_diag = top_diag
    columns_out = []
    cross_out = []
    diag_out = []
    for supernode in range(SN):
        slot_ids = slot_blocks[supernode]
        usable = slot_ids >= 0
        target = jnp.where(usable, slot_ids, 0).astype(jnp.int32)
        pieces = panel_blocks[supernode].reshape(N_PROW * SLOTS, BLK, W) * usable.astype(jnp.float32)[:, None, None]
        factor_rows = jnp.zeros((NA, BLK, W), jnp.float32).at[target].add(pieces).reshape(NA * BLK, W)
        factor_prev = prev_panel[supernode]
        combined = matmul(pool_inverse, factor_rows) + matmul(chain_column.T, factor_prev)
        fresh_column = -combined.T
        cross_block = -(matmul(chain_column, factor_rows) + matmul(chain_diag, factor_prev))
        diag_block = pivot_inverse[supernode] - (matmul(fresh_column, factor_rows) + matmul(cross_block.T, factor_prev))
        columns_out.append(fresh_column)
        cross_out.append(cross_block)
        diag_out.append(diag_block)
        chain_column = fresh_column
        chain_diag = diag_block
    return jnp.stack(columns_out), jnp.stack(cross_out), jnp.stack(diag_out)
```

```python
import functools

import jax
import jax.numpy as jnp
from jax import lax
from jax.experimental import pallas as pl
from jax.experimental.pallas import tpu as pltpu
from jax.sharding import PartitionSpec as P

BLK = 128
MESH = pl.DeviceIdType.MESH
CHUNKS = 4


def mm(left, right, dims=((1,), (0,))):
    return lax.dot_general(
        left, right, (dims, ((), ())), precision=lax.Precision.HIGHEST, preferred_element_type=jnp.float32
    )


def remote(src, dst, send_sem, recv_sem, device):
    return pltpu.make_async_remote_copy(
        src_ref=src, dst_ref=dst, send_sem=send_sem, recv_sem=recv_sem, device_id=device, device_id_type=MESH
    )


def kernel(
    rows, cols,
    slots, pool, panel, prev, pivot, top, diag,
    column_out, cross_out, diag_out,
    fbuf, lz, g, abuf, tbuf, csend, crecv, xbuf, cag, vsend, vrecv, dsend, drecv, dag,
    share_s, share_r, gup_s, gdn_s, gx_s, gz_r, gx_r, cs_s, cs_r, ca_s, ca_r, v_s, v_r, d_s, d_r, da_s, da_r,
):
    r = lax.axis_index("prow")
    c = lax.axis_index("pcol")
    ys = cols // 2
    y, k = c // 2, c % 2
    lines = rows // 2
    h, lo = r // 2, r % 2
    width = top.shape[0]
    thin = prev.shape[0]
    span = pool.shape[0]
    wide = prev.shape[1]
    half = wide // 2
    row_blocks = span // BLK
    n_slots = panel.shape[0] // BLK

    barrier = pltpu.get_barrier_semaphore()

    def greet(row, col):
        pl.semaphore_signal(barrier, inc=1, device_id=(row, col), device_id_type=MESH)

    home = r // 2 == c
    for i in range(1, rows):
        greet((r + i) % rows, c)
        greet((r + i) % rows, r // 2)
    for i in range(1, cols):
        greet(r, (c + i) % cols)
        for m in range(2):
            greet(2 * c + m, (c + i) % cols)

    @pl.when(r // 2 != c)
    def _():
        greet(r, r // 2)

    for m in range(2):
        @pl.when(r != 2 * c + m)
        def _(m=m):
            greet(2 * c + m, c)

    for b in range(row_blocks):
        block = jnp.zeros((BLK, wide), jnp.float32)
        for s in range(n_slots):
            used = jnp.where(slots[0, r * n_slots + s] == r * row_blocks + b, 1.0, 0.0)
            block = block + panel[pl.ds(s * BLK, BLK), :] * used
        fbuf[pl.ds(b * BLK, BLK), :] = block
    lz[...] = jnp.zeros_like(lz)
    lz[pl.ds(pl.multiple_of(r * thin, 8), thin), :] = prev[...]

    def own_columns(value):
        parts = [
            jnp.concatenate([value[:, (2 * q + kk) * width:(2 * q + kk + 1) * width] for q in range(ys)], 1)
            for kk in range(2)
        ]
        return jnp.where(k == 0, parts[0], parts[1])

    @pl.when(h // 2 == y)
    def _():
        mine = 2 * (h - 2 * y) + lo
        g[mine, pl.ds(0, span), :] = own_columns(fbuf[...])
        g[mine, pl.ds(span, thin), :] = own_columns(prev[...])

    abuf[k] = pool[...]
    tbuf[k] = top[...]

    others = 2 * rows + 3 * cols - 2
    pl.semaphore_wait(barrier, jnp.where(home, others - 2, others))

    peer = 1 - k

    step = span // CHUNKS
    pieces = [(i * step, step) for i in range(CHUNKS)] + [(span, thin)]

    def g_ref(b, low, n):
        return g.at[2 * b + low, pl.ds(pieces[n][0], pieces[n][1]), :]

    def up(b, n):
        return remote(g_ref(b, lo, n), g_ref(b, lo, n), gup_s.at[b, n], gz_r.at[b, n], (r + 2, c))

    def down(b, n):
        return remote(g_ref(b, lo, n), g_ref(b, lo, n), gdn_s.at[b, n], gz_r.at[b, n], (r - 2, c))

    def across(b, n):
        return remote(g_ref(b, lo, n), g_ref(b, lo, n), gx_s.at[b, n], gx_r.at[b, n], (r + 1 - 2 * lo, c))

    def forward(b, n):
        s = 2 * y + b

        @pl.when((h >= s) & (h + 1 < lines))
        def _():
            up(b, n).start()

        @pl.when((h <= s) & (h >= 1))
        def _():
            down(b, n).start()

        across(b, n).start()

    order = [len(pieces) - 1] + list(range(CHUNKS))
    for n in order:
        for b in range(2):
            @pl.when(h == 2 * y + b)
            def _(b=b, n=n):
                forward(b, n)

    share = [
        remote(abuf.at[k], abuf.at[k], share_s.at[0], share_r.at[0], (r, 2 * y + peer)),
        remote(tbuf.at[k], tbuf.at[k], share_s.at[1], share_r.at[1], (r, 2 * y + peer)),
    ]
    for copy in share:
        copy.start()

    cross = mm(top[...], fbuf[...]) + mm(diag[...], lz[...])
    for m in range(2):
        for q in range(cols):
            csend[m * cols + q] = cross[m * thin:(m + 1) * thin, q * width:(q + 1) * width]

    def scatter(m, i):
        q = (c + i) % cols
        return remote(csend.at[m * cols + q], crecv.at[r], cs_s.at[m, i], cs_r.at[r], (2 * c + m, q))

    for i in range(1, cols):
        for m in range(2):
            scatter(m, i).start()
    for m in range(2):
        @pl.when(r != 2 * c + m)
        def _(m=m):
            scatter(m, 0).start()

        @pl.when(r == 2 * c + m)
        def _(m=m):
            crecv[r] = csend[m * cols + c]

    for n in order:
        for b in range(2):
            @pl.when(h != 2 * y + b)
            def _(b=b, n=n):
                up(b, n).wait_recv()
                forward(b, n)

    for i in range(1, rows):
        p = (r + i) % rows
        remote(crecv.at[p], crecv.at[p], cs_s.at[0, 0], cs_r.at[p], (p, c)).wait_recv()

    @pl.when(r // 2 != c)
    def _():
        remote(crecv.at[r], crecv.at[r], cs_s.at[0, 0], cs_r.at[r], (r, r // 2)).wait_recv()

    total = crecv[0]
    for p in range(1, rows):
        total = total + crecv[p]
    xbuf[...] = -total
    mine_slot = (r % 2) * cols + c

    def gather_cross(i):
        p = (r + i) % rows
        return remote(xbuf, cag.at[mine_slot], ca_s.at[i], ca_r.at[mine_slot], (p, r // 2))

    for i in range(1, rows):
        gather_cross(i).start()

    @pl.when(r // 2 != c)
    def _():
        gather_cross(0).start()

    @pl.when(r // 2 == c)
    def _():
        cag[mine_slot] = xbuf[...]

    for copy in share:
        copy.wait_recv()
    for n in order:
        for b in range(2):
            low = 1 - lo
            remote(g_ref(b, low, n), g_ref(b, low, n), gx_s.at[b, n], gx_r.at[b, n], (r + 1 - 2 * lo, c)).wait_recv()
    part = jnp.zeros((span, half), jnp.float32)
    for kk in range(2):
        for m in range(2):
            j = 2 * kk + m
            part = part + mm(abuf[kk, :, m * span:(m + 1) * span], g[j, pl.ds(0, span), :])
            part = part + mm(
                tbuf[kk, pl.ds(m * thin, thin), :], g[j, pl.ds(span, thin), :], ((0,), (0,))
            )
    for q in range(ys):
        vsend[q] = part[:, q * width:(q + 1) * width]

    def scatter_v(i):
        q = (y + i) % ys
        return remote(vsend.at[q], vrecv.at[y], v_s.at[i], v_r.at[y], (r, 2 * q + k))

    for i in range(1, ys):
        scatter_v(i).start()
    second = mm(xbuf[...], prev[...], ((0,), (0,)))
    total = vsend[y]
    for i in range(1, ys):
        q = (y + i) % ys
        remote(vrecv.at[q], vrecv.at[q], v_s.at[i], v_r.at[q], (r, 2 * q + k)).wait_recv()
        total = total + vrecv[q]
    column = -total.T
    column_out[...] = column

    term = mm(column, fbuf[...]) + second
    slab = width // rows
    for p in range(rows):
        dsend[p] = term[p * slab:(p + 1) * slab, :]

    def scatter_d(i):
        p = (r + i) % rows
        return remote(dsend.at[p], drecv.at[r], d_s.at[i], d_r.at[r], (p, c))

    for i in range(1, rows):
        scatter_d(i).start()
    total = dsend[r]
    for i in range(1, rows):
        p = (r + i) % rows
        remote(drecv.at[p], drecv.at[p], d_s.at[i], d_r.at[p], (p, c)).wait_recv()
        total = total + drecv[p]
    dag[r] = pivot[r] - total

    def gather_d(i):
        p = (r + i) % rows
        return remote(dag.at[r], dag.at[r], da_s.at[i], da_r.at[r], (p, c))

    for i in range(1, rows):
        gather_d(i).start()

    for i in range(1, cols):
        for m in range(2):
            slot = m * cols + (c + i) % cols
            remote(cag.at[slot], cag.at[slot], ca_s.at[0], ca_r.at[slot], (2 * c + m, (c + i) % cols)).wait_recv()
    for m in range(2):
        @pl.when(r != 2 * c + m)
        def _(m=m):
            slot = m * cols + c
            remote(cag.at[slot], cag.at[slot], ca_s.at[0], ca_r.at[slot], (2 * c + m, c)).wait_recv()
    for m in range(2):
        for q in range(cols):
            cross_out[pl.ds(m * thin, thin), pl.ds(q * width, width)] = cag[m * cols + q]

    for i in range(1, rows):
        p = (r + i) % rows
        remote(dag.at[p], dag.at[p], da_s.at[i], da_r.at[p], (p, c)).wait_recv()
    diag_out[...] = dag[...]

    for copy in share:
        copy.wait_send()
    for n in order:
        for b in range(2):
            s = 2 * y + b

            @pl.when((h >= s) & (h + 1 < lines))
            def _(b=b, n=n):
                up(b, n).wait_send()

            @pl.when((h <= s) & (h >= 1))
            def _(b=b, n=n):
                down(b, n).wait_send()

            across(b, n).wait_send()
    for i in range(1, cols):
        for m in range(2):
            scatter(m, i).wait_send()
    for m in range(2):
        @pl.when(r != 2 * c + m)
        def _(m=m):
            scatter(m, 0).wait_send()
    for i in range(1, rows):
        gather_cross(i).wait_send()

    @pl.when(r // 2 != c)
    def _():
        gather_cross(0).wait_send()

    for i in range(1, ys):
        scatter_v(i).wait_send()
    for i in range(1, rows):
        scatter_d(i).wait_send()
        gather_d(i).wait_send()


def solution(mesh):
    rows, cols = mesh.shape["prow"], mesh.shape["pcol"]
    ys = cols // 2

    def body(pool, panel, prev, pivot, top, diag, slots):
        panel, prev, pivot = panel[0], prev[0], pivot[0]
        span = pool.shape[0]
        width = top.shape[0]
        thin, wide = prev.shape
        half = wide // 2
        slab = width // rows
        f32 = jnp.float32
        vm = pl.BlockSpec(memory_space=pltpu.VMEM)
        dma = pltpu.SemaphoreType.DMA
        n = CHUNKS + 1
        column, cross, new_diag = pl.pallas_call(
            functools.partial(kernel, rows, cols),
            out_shape=(
                jax.ShapeDtypeStruct((width, span), f32),
                jax.ShapeDtypeStruct((width, wide), f32),
                jax.ShapeDtypeStruct((rows, slab, wide), f32),
            ),
            in_specs=[pl.BlockSpec(memory_space=pltpu.SMEM)] + [vm] * 6,
            out_specs=(vm, vm, vm),
            scratch_shapes=[
                pltpu.VMEM((span, wide), f32),
                pltpu.VMEM((wide, wide), f32),
                pltpu.VMEM((4, span + thin, half), f32),
                pltpu.VMEM((2,) + pool.shape, f32),
                pltpu.VMEM((2, width, span), f32),
                pltpu.VMEM((2 * cols, thin, width), f32),
                pltpu.VMEM((rows, thin, width), f32),
                pltpu.VMEM((thin, width), f32),
                pltpu.VMEM((2 * cols, thin, width), f32),
                pltpu.VMEM((ys, span, width), f32),
                pltpu.VMEM((ys, span, width), f32),
                pltpu.VMEM((rows, slab, wide), f32),
                pltpu.VMEM((rows, slab, wide), f32),
                pltpu.VMEM((rows, slab, wide), f32),
                dma((2,)), dma((2,)),
                dma((2, n)), dma((2, n)), dma((2, n)), dma((2, n)), dma((2, n)),
                dma((2, cols)), dma((rows,)), dma((rows,)), dma((2 * cols,)),
                dma((ys,)), dma((ys,)),
                dma((rows,)), dma((rows,)), dma((rows,)), dma((rows,)),
            ],
            compiler_params=pltpu.CompilerParams(
                collective_id=0, has_side_effects=True, vmem_limit_bytes=40 * 2**20
            ),
        )(slots, pool, panel, prev, pivot.reshape(rows, slab, wide), top, diag)
        return column[None], cross[None], new_diag.reshape(1, width, wide)

    in_specs = (
        P("prow", "pcol"),
        P(None, "prow", None),
        P(None, "prow", None),
        P(None, "pcol", None),
        P("pcol", "prow"),
        P("pcol", None),
        P(),
    )
    out_specs = (P(None, "pcol", "prow"), P(None, "pcol", None), P(None, "pcol", None))
    return jax.shard_map(body, mesh=mesh, in_specs=in_specs, out_specs=out_specs, check_vma=False)
```

```python
import functools

import jax
import jax.numpy as jnp
from jax import lax
from jax.experimental import pallas as pl
from jax.experimental.pallas import tpu as pltpu
from jax.sharding import PartitionSpec as P

BLK = 128
MESH = pl.DeviceIdType.MESH
CHUNKS = 4


def mm(left, right, dims=((1,), (0,))):
    return lax.dot_general(
        left, right, (dims, ((), ())), precision=lax.Precision.HIGHEST, preferred_element_type=jnp.float32
    )


def remote(src, dst, send_sem, recv_sem, device):
    return pltpu.make_async_remote_copy(
        src_ref=src, dst_ref=dst, send_sem=send_sem, recv_sem=recv_sem, device_id=device, device_id_type=MESH
    )


def kernel(
    rows, cols,
    slots, pool_in, panel_in, prev_in, pivot_in, top_in, diag_in,
    column_out, cross_out, diag_out,
    panel, prev, pivot, top, diag, load_s,
    fbuf, lz, g, abuf, tbuf, csend, crecv, xbuf, cag, vsend, vrecv, dsend, drecv, dag,
    share_s, share_r, gup_s, gdn_s, gx_s, gz_r, gx_r, cs_s, cs_r, ca_s, ca_r, v_s, v_r, d_s, d_r, da_s, da_r,
):
    r = lax.axis_index("prow")
    c = lax.axis_index("pcol")
    ys = cols // 2
    y, k = c // 2, c % 2
    lines = rows // 2
    h, lo = r // 2, r % 2
    loads = [
        pltpu.make_async_copy(src, dst, load_s.at[i])
        for i, (src, dst) in enumerate([
            (panel_in, panel), (prev_in, prev), (top_in, top), (diag_in, diag),
            (pivot_in, pivot), (pool_in, abuf.at[k]), (top_in, tbuf.at[k]),
        ])
    ]
    for load in loads:
        load.start()
    width = top.shape[0]
    thin = prev.shape[0]
    span = pool_in.shape[0]
    wide = prev.shape[1]
    half = wide // 2
    row_blocks = span // BLK
    n_slots = panel.shape[0] // BLK

    barrier = pltpu.get_barrier_semaphore()

    def greet(row, col):
        pl.semaphore_signal(barrier, inc=1, device_id=(row, col), device_id_type=MESH)

    home = r // 2 == c
    for i in range(1, rows):
        greet((r + i) % rows, c)
        greet((r + i) % rows, r // 2)
    for i in range(1, cols):
        greet(r, (c + i) % cols)
        for m in range(2):
            greet(2 * c + m, (c + i) % cols)

    @pl.when(r // 2 != c)
    def _():
        greet(r, r // 2)

    for m in range(2):
        @pl.when(r != 2 * c + m)
        def _(m=m):
            greet(2 * c + m, c)

    loads[0].wait()
    loads[1].wait()

    for b in range(row_blocks):
        block = jnp.zeros((BLK, wide), jnp.float32)
        for s in range(n_slots):
            used = jnp.where(slots[0, r * n_slots + s] == r * row_blocks + b, 1.0, 0.0)
            block = block + panel[pl.ds(s * BLK, BLK), :] * used
        fbuf[pl.ds(b * BLK, BLK), :] = block
    lz[...] = jnp.zeros_like(lz)
    lz[pl.ds(pl.multiple_of(r * thin, 8), thin), :] = prev[...]

    def own_columns(value):
        parts = [
            jnp.concatenate([value[:, (2 * q + kk) * width:(2 * q + kk + 1) * width] for q in range(ys)], 1)
            for kk in range(2)
        ]
        return jnp.where(k == 0, parts[0], parts[1])

    @pl.when(h // 2 == y)
    def _():
        mine = 2 * (h - 2 * y) + lo
        g[mine, pl.ds(0, span), :] = own_columns(fbuf[...])
        g[mine, pl.ds(span, thin), :] = own_columns(prev[...])

    others = 2 * rows + 3 * cols - 2
    pl.semaphore_wait(barrier, jnp.where(home, others - 2, others))

    peer = 1 - k

    step = span // CHUNKS
    pieces = [(i * step, step) for i in range(CHUNKS)] + [(span, thin)]

    def g_ref(b, low, n):
        return g.at[2 * b + low, pl.ds(pieces[n][0], pieces[n][1]), :]

    def up(b, n):
        return remote(g_ref(b, lo, n), g_ref(b, lo, n), gup_s.at[b, n], gz_r.at[b, n], (r + 2, c))

    def down(b, n):
        return remote(g_ref(b, lo, n), g_ref(b, lo, n), gdn_s.at[b, n], gz_r.at[b, n], (r - 2, c))

    def across(b, n):
        return remote(g_ref(b, lo, n), g_ref(b, lo, n), gx_s.at[b, n], gx_r.at[b, n], (r + 1 - 2 * lo, c))

    def forward(b, n):
        s = 2 * y + b

        @pl.when((h >= s) & (h + 1 < lines))
        def _():
            up(b, n).start()

        @pl.when((h <= s) & (h >= 1))
        def _():
            down(b, n).start()

        across(b, n).start()

    order = [len(pieces) - 1] + list(range(CHUNKS))
    near = jnp.clip(h - 2 * y, 0, 1)
    far = 1 - near
    source = h == 2 * y + near
    for n in order:
        @pl.when(source)
        def _(n=n):
            forward(near, n)

    share = [
        remote(pool_in, abuf.at[k], share_s.at[0], share_r.at[0], (r, 2 * y + peer)),
        remote(top_in, tbuf.at[k], share_s.at[1], share_r.at[1], (r, 2 * y + peer)),
    ]
    for copy in share:
        copy.start()

    loads[2].wait()
    loads[3].wait()
    cross = mm(top[...], fbuf[...]) + mm(diag[...], lz[...])
    for m in range(2):
        for q in range(cols):
            csend[m * cols + q] = cross[m * thin:(m + 1) * thin, q * width:(q + 1) * width]

    def scatter(m, i):
        q = (c + i) % cols
        return remote(csend.at[m * cols + q], crecv.at[r], cs_s.at[m, i], cs_r.at[r], (2 * c + m, q))

    for i in range(1, cols):
        for m in range(2):
            scatter(m, i).start()
    for m in range(2):
        @pl.when(r != 2 * c + m)
        def _(m=m):
            scatter(m, 0).start()

        @pl.when(r == 2 * c + m)
        def _(m=m):
            crecv[r] = csend[m * cols + c]

    def product(b, low):
        j = 2 * b + low
        left = abuf[b, :, pl.ds(pl.multiple_of(low * span, BLK), span)]
        out = mm(left, g[j, pl.ds(0, span), :])
        return out + mm(
            tbuf[b, pl.ds(pl.multiple_of(low * thin, 8), thin), :], g[j, pl.ds(span, thin), :], ((0,), (0,))
        )

    for n in order:
        @pl.when(jnp.logical_not(source))
        def _(n=n):
            up(near, n).wait_recv()
            forward(near, n)

    part = None
    for at, n in enumerate(order):
        up(far, n).wait_recv()
        forward(far, n)
        if at == 1:
            for load in loads[4:]:
                load.wait()
            for copy in share:
                copy.wait_recv()
            part = product(near, lo)

    for i in range(1, rows):
        p = (r + i) % rows
        remote(crecv.at[p], crecv.at[p], cs_s.at[0, 0], cs_r.at[p], (p, c)).wait_recv()

    @pl.when(r // 2 != c)
    def _():
        remote(crecv.at[r], crecv.at[r], cs_s.at[0, 0], cs_r.at[r], (r, r // 2)).wait_recv()

    total = crecv[0]
    for p in range(1, rows):
        total = total + crecv[p]
    xbuf[...] = -total
    mine_slot = (r % 2) * cols + c

    def gather_cross(i):
        p = (r + i) % rows
        return remote(xbuf, cag.at[mine_slot], ca_s.at[i], ca_r.at[mine_slot], (p, r // 2))

    for i in range(1, rows):
        gather_cross(i).start()

    @pl.when(r // 2 != c)
    def _():
        gather_cross(0).start()

    @pl.when(r // 2 == c)
    def _():
        cag[mine_slot] = xbuf[...]

    part = part + product(far, lo)
    for b in (near, far):
        for n in order:
            low = 1 - lo
            remote(g_ref(b, low, n), g_ref(b, low, n), gx_s.at[b, n], gx_r.at[b, n], (r + 1 - 2 * lo, c)).wait_recv()
        part = part + product(b, 1 - lo)
    for q in range(ys):
        vsend[q] = part[:, q * width:(q + 1) * width]

    def scatter_v(i):
        q = (y + i) % ys
        return remote(vsend.at[q], vrecv.at[y], v_s.at[i], v_r.at[y], (r, 2 * q + k))

    for i in range(1, ys):
        scatter_v(i).start()
    second = mm(xbuf[...], prev[...], ((0,), (0,)))
    total = vsend[y]
    for i in range(1, ys):
        q = (y + i) % ys
        remote(vrecv.at[q], vrecv.at[q], v_s.at[i], v_r.at[q], (r, 2 * q + k)).wait_recv()
        total = total + vrecv[q]
    column = -total.T
    column_out[...] = column

    term = mm(column, fbuf[...]) + second
    slab = width // rows
    for p in range(rows):
        dsend[p] = term[p * slab:(p + 1) * slab, :]

    def scatter_d(i):
        p = (r + i) % rows
        return remote(dsend.at[p], drecv.at[r], d_s.at[i], d_r.at[r], (p, c))

    for i in range(1, rows):
        scatter_d(i).start()
    total = dsend[r]
    for i in range(1, rows):
        p = (r + i) % rows
        remote(drecv.at[p], drecv.at[p], d_s.at[i], d_r.at[p], (p, c)).wait_recv()
        total = total + drecv[p]
    dag[r] = pivot[r] - total

    def gather_d(i):
        p = (r + i) % rows
        return remote(dag.at[r], dag.at[r], da_s.at[i], da_r.at[r], (p, c))

    for i in range(1, rows):
        gather_d(i).start()

    for i in range(1, cols):
        for m in range(2):
            slot = m * cols + (c + i) % cols
            remote(cag.at[slot], cag.at[slot], ca_s.at[0], ca_r.at[slot], (2 * c + m, (c + i) % cols)).wait_recv()
    for m in range(2):
        @pl.when(r != 2 * c + m)
        def _(m=m):
            slot = m * cols + c
            remote(cag.at[slot], cag.at[slot], ca_s.at[0], ca_r.at[slot], (2 * c + m, c)).wait_recv()
    for m in range(2):
        for q in range(cols):
            cross_out[pl.ds(m * thin, thin), pl.ds(q * width, width)] = cag[m * cols + q]

    for i in range(1, rows):
        p = (r + i) % rows
        remote(dag.at[p], dag.at[p], da_s.at[i], da_r.at[p], (p, c)).wait_recv()
    diag_out[...] = dag[...]

    for copy in share:
        copy.wait_send()
    for n in order:
        for b in range(2):
            s = 2 * y + b

            @pl.when((h >= s) & (h + 1 < lines))
            def _(b=b, n=n):
                up(b, n).wait_send()

            @pl.when((h <= s) & (h >= 1))
            def _(b=b, n=n):
                down(b, n).wait_send()

            across(b, n).wait_send()
    for i in range(1, cols):
        for m in range(2):
            scatter(m, i).wait_send()
    for m in range(2):
        @pl.when(r != 2 * c + m)
        def _(m=m):
            scatter(m, 0).wait_send()
    for i in range(1, rows):
        gather_cross(i).wait_send()

    @pl.when(r // 2 != c)
    def _():
        gather_cross(0).wait_send()

    for i in range(1, ys):
        scatter_v(i).wait_send()
    for i in range(1, rows):
        scatter_d(i).wait_send()
        gather_d(i).wait_send()


def solution(mesh):
    rows, cols = mesh.shape["prow"], mesh.shape["pcol"]
    ys = cols // 2

    def body(pool, panel, prev, pivot, top, diag, slots):
        panel, prev, pivot = panel[0], prev[0], pivot[0]
        span = pool.shape[0]
        width = top.shape[0]
        thin, wide = prev.shape
        half = wide // 2
        slab = width // rows
        f32 = jnp.float32
        vm = pl.BlockSpec(memory_space=pltpu.VMEM)
        dma = pltpu.SemaphoreType.DMA
        n = CHUNKS + 1
        column, cross, new_diag = pl.pallas_call(
            functools.partial(kernel, rows, cols),
            out_shape=(
                jax.ShapeDtypeStruct((width, span), f32),
                jax.ShapeDtypeStruct((width, wide), f32),
                jax.ShapeDtypeStruct((rows, slab, wide), f32),
            ),
            in_specs=[pl.BlockSpec(memory_space=pltpu.SMEM)] + [pl.BlockSpec(memory_space=pltpu.HBM)] * 6,
            out_specs=(vm, vm, vm),
            scratch_shapes=[
                pltpu.VMEM(panel.shape, f32),
                pltpu.VMEM(prev.shape, f32),
                pltpu.VMEM((rows, slab, wide), f32),
                pltpu.VMEM(top.shape, f32),
                pltpu.VMEM(diag.shape, f32),
                dma((7,)),
                pltpu.VMEM((span, wide), f32),
                pltpu.VMEM((wide, wide), f32),
                pltpu.VMEM((4, span + thin, half), f32),
                pltpu.VMEM((2,) + pool.shape, f32),
                pltpu.VMEM((2, width, span), f32),
                pltpu.VMEM((2 * cols, thin, width), f32),
                pltpu.VMEM((rows, thin, width), f32),
                pltpu.VMEM((thin, width), f32),
                pltpu.VMEM((2 * cols, thin, width), f32),
                pltpu.VMEM((ys, span, width), f32),
                pltpu.VMEM((ys, span, width), f32),
                pltpu.VMEM((rows, slab, wide), f32),
                pltpu.VMEM((rows, slab, wide), f32),
                pltpu.VMEM((rows, slab, wide), f32),
                dma((2,)), dma((2,)),
                dma((2, n)), dma((2, n)), dma((2, n)), dma((2, n)), dma((2, n)),
                dma((2, cols)), dma((rows,)), dma((rows,)), dma((2 * cols,)),
                dma((ys,)), dma((ys,)),
                dma((rows,)), dma((rows,)), dma((rows,)), dma((rows,)),
            ],
            compiler_params=pltpu.CompilerParams(
                collective_id=0, has_side_effects=True, vmem_limit_bytes=60 * 2**20
            ),
        )(slots, pool, panel, prev, pivot.reshape(rows, slab, wide), top, diag)
        return column[None], cross[None], new_diag.reshape(1, width, wide)

    in_specs = (
        P("prow", "pcol"),
        P(None, "prow", None),
        P(None, "prow", None),
        P(None, "pcol", None),
        P("pcol", "prow"),
        P("pcol", None),
        P(),
    )
    out_specs = (P(None, "pcol", "prow"), P(None, "pcol", None), P(None, "pcol", None))
    return jax.shard_map(body, mesh=mesh, in_specs=in_specs, out_specs=out_specs, check_vma=False)
```

```python
import functools

import jax
import jax.numpy as jnp
from jax import lax
from jax.experimental import pallas as pl
from jax.experimental.pallas import tpu as pltpu
from jax.sharding import PartitionSpec as P

BLK = 128
MESH = pl.DeviceIdType.MESH
CHUNKS = 8


def halves(value):
    high = value.astype(jnp.bfloat16)
    return high, (value - high.astype(jnp.float32)).astype(jnp.bfloat16)


def mm(left, right, dims=((1,), (0,))):
    def dot(a, b):
        return lax.dot_general(a, b, (dims, ((), ())), preferred_element_type=jnp.float32)

    left_high, left_low = halves(left)
    right_high, right_low = halves(right)
    return dot(left_high, right_high) + (dot(left_high, right_low) + dot(left_low, right_high))


def remote(src, dst, send_sem, recv_sem, device):
    return pltpu.make_async_remote_copy(
        src_ref=src, dst_ref=dst, send_sem=send_sem, recv_sem=recv_sem, device_id=device, device_id_type=MESH
    )


def kernel(
    rows, cols,
    slots, pool_in, panel_in, prev_in, pivot_in, top_in, diag_in,
    column_out, cross_out, diag_out,
    panel, prev, pivot, top, diag, load_s,
    fbuf, lz, g, abuf, tbuf, csend, crecv, xbuf, cag, vsend, vrecv, dsend, drecv, dag,
    share_s, share_r, gup_s, gdn_s, gx_s, gz_r, gx_r, cs_s, cs_r, ca_s, ca_r, v_s, v_r, d_s, d_r, da_s, da_r,
):
    r = lax.axis_index("prow")
    c = lax.axis_index("pcol")
    ys = cols // 2
    y, k = c // 2, c % 2
    lines = rows // 2
    h, lo = r // 2, r % 2
    loads = [
        pltpu.make_async_copy(src, dst, load_s.at[i])
        for i, (src, dst) in enumerate([
            (panel_in, panel), (prev_in, prev), (top_in, top), (diag_in, diag),
            (pivot_in, pivot), (pool_in, abuf.at[k]), (top_in, tbuf.at[k]),
        ])
    ]
    for load in loads:
        load.start()
    width = top.shape[0]
    thin = prev.shape[0]
    span = pool_in.shape[0]
    wide = prev.shape[1]
    half = wide // 2
    row_blocks = span // BLK
    n_slots = panel.shape[0] // BLK

    barrier = pltpu.get_barrier_semaphore()

    def greet(row, col):
        pl.semaphore_signal(barrier, inc=1, device_id=(row, col), device_id_type=MESH)

    home = r // 2 == c
    for i in range(1, rows):
        greet((r + i) % rows, c)
        greet((r + i) % rows, r // 2)
    for i in range(1, cols):
        greet(r, (c + i) % cols)
        for m in range(2):
            greet(2 * c + m, (c + i) % cols)

    @pl.when(r // 2 != c)
    def _():
        greet(r, r // 2)

    for m in range(2):
        @pl.when(r != 2 * c + m)
        def _(m=m):
            greet(2 * c + m, c)

    loads[0].wait()
    loads[1].wait()

    for b in range(row_blocks):
        block = jnp.zeros((BLK, wide), jnp.float32)
        for s in range(n_slots):
            used = jnp.where(slots[0, r * n_slots + s] == r * row_blocks + b, 1.0, 0.0)
            block = block + panel[pl.ds(s * BLK, BLK), :] * used
        fbuf[pl.ds(b * BLK, BLK), :] = block
    lz[...] = jnp.zeros_like(lz)
    lz[pl.ds(pl.multiple_of(r * thin, 8), thin), :] = prev[...]

    def own_columns(value):
        parts = [
            jnp.concatenate([value[:, (2 * q + kk) * width:(2 * q + kk + 1) * width] for q in range(ys)], 1)
            for kk in range(2)
        ]
        return jnp.where(k == 0, parts[0], parts[1])

    @pl.when(h // 2 == y)
    def _():
        mine = 2 * (h - 2 * y) + lo
        g[mine, pl.ds(0, span), :] = own_columns(fbuf[...])
        g[mine, pl.ds(span, thin), :] = own_columns(prev[...])

    others = 2 * rows + 3 * cols - 2
    pl.semaphore_wait(barrier, jnp.where(home, others - 2, others))

    peer = 1 - k

    step = span // CHUNKS
    pieces = [(i * step, step) for i in range(CHUNKS)] + [(span, thin)]

    def g_ref(b, low, n):
        return g.at[2 * b + low, pl.ds(pieces[n][0], pieces[n][1]), :]

    def up(b, n):
        return remote(g_ref(b, lo, n), g_ref(b, lo, n), gup_s.at[b, n], gz_r.at[b, n], (r + 2, c))

    def down(b, n):
        return remote(g_ref(b, lo, n), g_ref(b, lo, n), gdn_s.at[b, n], gz_r.at[b, n], (r - 2, c))

    def across(b, n):
        return remote(g_ref(b, lo, n), g_ref(b, lo, n), gx_s.at[b, n], gx_r.at[b, n], (r + 1 - 2 * lo, c))

    def forward(b, n):
        s = 2 * y + b

        @pl.when((h >= s) & (h + 1 < lines))
        def _():
            up(b, n).start()

        @pl.when((h <= s) & (h >= 1))
        def _():
            down(b, n).start()

        across(b, n).start()

    order = [len(pieces) - 1] + list(range(CHUNKS))
    near = jnp.clip(h - 2 * y, 0, 1)
    far = 1 - near
    source = h == 2 * y + near
    for n in order:
        @pl.when(source)
        def _(n=n):
            forward(near, n)

    share = [
        remote(pool_in, abuf.at[k], share_s.at[0], share_r.at[0], (r, 2 * y + peer)),
        remote(top_in, tbuf.at[k], share_s.at[1], share_r.at[1], (r, 2 * y + peer)),
    ]
    for copy in share:
        copy.start()

    loads[2].wait()
    loads[3].wait()
    cross = mm(top[...], fbuf[...]) + mm(diag[...], lz[...])
    for m in range(2):
        for q in range(cols):
            csend[m * cols + q] = cross[m * thin:(m + 1) * thin, q * width:(q + 1) * width]

    def scatter(m, i):
        q = (c + i) % cols
        return remote(csend.at[m * cols + q], crecv.at[r], cs_s.at[m, i], cs_r.at[r], (2 * c + m, q))

    for i in range(1, cols):
        for m in range(2):
            scatter(m, i).start()
    for m in range(2):
        @pl.when(r != 2 * c + m)
        def _(m=m):
            scatter(m, 0).start()

        @pl.when(r == 2 * c + m)
        def _(m=m):
            crecv[r] = csend[m * cols + c]

    def product(b, low):
        j = 2 * b + low
        left = abuf[b, :, pl.ds(pl.multiple_of(low * span, BLK), span)]
        out = mm(left, g[j, pl.ds(0, span), :])
        return out + mm(
            tbuf[b, pl.ds(pl.multiple_of(low * thin, 8), thin), :], g[j, pl.ds(span, thin), :], ((0,), (0,))
        )

    for n in order:
        @pl.when(jnp.logical_not(source))
        def _(n=n):
            up(near, n).wait_recv()
            forward(near, n)

    part = None
    for at, n in enumerate(order):
        up(far, n).wait_recv()
        forward(far, n)
        if at == 1:
            for load in loads[4:]:
                load.wait()
            for copy in share:
                copy.wait_recv()
            part = product(near, lo)

    for i in range(1, rows):
        p = (r + i) % rows
        remote(crecv.at[p], crecv.at[p], cs_s.at[0, 0], cs_r.at[p], (p, c)).wait_recv()

    @pl.when(r // 2 != c)
    def _():
        remote(crecv.at[r], crecv.at[r], cs_s.at[0, 0], cs_r.at[r], (r, r // 2)).wait_recv()

    total = crecv[0]
    for p in range(1, rows):
        total = total + crecv[p]
    xbuf[...] = -total
    mine_slot = (r % 2) * cols + c

    def gather_cross(i):
        p = (r + i) % rows
        return remote(xbuf, cag.at[mine_slot], ca_s.at[i], ca_r.at[mine_slot], (p, r // 2))

    for i in range(1, rows):
        gather_cross(i).start()

    @pl.when(r // 2 != c)
    def _():
        gather_cross(0).start()

    @pl.when(r // 2 == c)
    def _():
        cag[mine_slot] = xbuf[...]

    part = part + product(far, lo)
    for b in (near, far):
        for n in order:
            low = 1 - lo
            remote(g_ref(b, low, n), g_ref(b, low, n), gx_s.at[b, n], gx_r.at[b, n], (r + 1 - 2 * lo, c)).wait_recv()
        part = part + product(b, 1 - lo)
    for q in range(ys):
        vsend[q] = part[:, q * width:(q + 1) * width]

    def scatter_v(i):
        q = (y + i) % ys
        return remote(vsend.at[q], vrecv.at[y], v_s.at[i], v_r.at[y], (r, 2 * q + k))

    for i in range(1, ys):
        scatter_v(i).start()
    second = mm(xbuf[...], prev[...], ((0,), (0,)))
    total = vsend[y]
    for i in range(1, ys):
        q = (y + i) % ys
        remote(vrecv.at[q], vrecv.at[q], v_s.at[i], v_r.at[q], (r, 2 * q + k)).wait_recv()
        total = total + vrecv[q]
    column = -total.T
    column_out[...] = column

    term = mm(column, fbuf[...]) + second
    slab = width // rows
    for p in range(rows):
        dsend[p] = term[p * slab:(p + 1) * slab, :]

    def scatter_d(i):
        p = (r + i) % rows
        return remote(dsend.at[p], drecv.at[r], d_s.at[i], d_r.at[r], (p, c))

    for i in range(1, rows):
        scatter_d(i).start()
    total = dsend[r]
    for i in range(1, rows):
        p = (r + i) % rows
        remote(drecv.at[p], drecv.at[p], d_s.at[i], d_r.at[p], (p, c)).wait_recv()
        total = total + drecv[p]
    dag[r] = pivot[r] - total

    def gather_d(i):
        p = (r + i) % rows
        return remote(dag.at[r], dag.at[r], da_s.at[i], da_r.at[r], (p, c))

    for i in range(1, rows):
        gather_d(i).start()

    for i in range(1, cols):
        for m in range(2):
            slot = m * cols + (c + i) % cols
            remote(cag.at[slot], cag.at[slot], ca_s.at[0], ca_r.at[slot], (2 * c + m, (c + i) % cols)).wait_recv()
    for m in range(2):
        @pl.when(r != 2 * c + m)
        def _(m=m):
            slot = m * cols + c
            remote(cag.at[slot], cag.at[slot], ca_s.at[0], ca_r.at[slot], (2 * c + m, c)).wait_recv()
    for m in range(2):
        for q in range(cols):
            cross_out[pl.ds(m * thin, thin), pl.ds(q * width, width)] = cag[m * cols + q]

    for i in range(1, rows):
        p = (r + i) % rows
        remote(dag.at[p], dag.at[p], da_s.at[i], da_r.at[p], (p, c)).wait_recv()
    diag_out[...] = dag[...]

    for copy in share:
        copy.wait_send()
    for n in order:
        for b in range(2):
            s = 2 * y + b

            @pl.when((h >= s) & (h + 1 < lines))
            def _(b=b, n=n):
                up(b, n).wait_send()

            @pl.when((h <= s) & (h >= 1))
            def _(b=b, n=n):
                down(b, n).wait_send()

            across(b, n).wait_send()
    for i in range(1, cols):
        for m in range(2):
            scatter(m, i).wait_send()
    for m in range(2):
        @pl.when(r != 2 * c + m)
        def _(m=m):
            scatter(m, 0).wait_send()
    for i in range(1, rows):
        gather_cross(i).wait_send()

    @pl.when(r // 2 != c)
    def _():
        gather_cross(0).wait_send()

    for i in range(1, ys):
        scatter_v(i).wait_send()
    for i in range(1, rows):
        scatter_d(i).wait_send()
        gather_d(i).wait_send()


def solution(mesh):
    rows, cols = mesh.shape["prow"], mesh.shape["pcol"]
    ys = cols // 2

    def body(pool, panel, prev, pivot, top, diag, slots):
        panel, prev, pivot = panel[0], prev[0], pivot[0]
        span = pool.shape[0]
        width = top.shape[0]
        thin, wide = prev.shape
        half = wide // 2
        slab = width // rows
        f32 = jnp.float32
        vm = pl.BlockSpec(memory_space=pltpu.VMEM)
        dma = pltpu.SemaphoreType.DMA
        n = CHUNKS + 1
        column, cross, new_diag = pl.pallas_call(
            functools.partial(kernel, rows, cols),
            out_shape=(
                jax.ShapeDtypeStruct((width, span), f32),
                jax.ShapeDtypeStruct((width, wide), f32),
                jax.ShapeDtypeStruct((rows, slab, wide), f32),
            ),
            in_specs=[pl.BlockSpec(memory_space=pltpu.SMEM)] + [pl.BlockSpec(memory_space=pltpu.HBM)] * 6,
            out_specs=(vm, vm, vm),
            scratch_shapes=[
                pltpu.VMEM(panel.shape, f32),
                pltpu.VMEM(prev.shape, f32),
                pltpu.VMEM((rows, slab, wide), f32),
                pltpu.VMEM(top.shape, f32),
                pltpu.VMEM(diag.shape, f32),
                dma((7,)),
                pltpu.VMEM((span, wide), f32),
                pltpu.VMEM((wide, wide), f32),
                pltpu.VMEM((4, span + thin, half), f32),
                pltpu.VMEM((2,) + pool.shape, f32),
                pltpu.VMEM((2, width, span), f32),
                pltpu.VMEM((2 * cols, thin, width), f32),
                pltpu.VMEM((rows, thin, width), f32),
                pltpu.VMEM((thin, width), f32),
                pltpu.VMEM((2 * cols, thin, width), f32),
                pltpu.VMEM((ys, span, width), f32),
                pltpu.VMEM((ys, span, width), f32),
                pltpu.VMEM((rows, slab, wide), f32),
                pltpu.VMEM((rows, slab, wide), f32),
                pltpu.VMEM((rows, slab, wide), f32),
                dma((2,)), dma((2,)),
                dma((2, n)), dma((2, n)), dma((2, n)), dma((2, n)), dma((2, n)),
                dma((2, cols)), dma((rows,)), dma((rows,)), dma((2 * cols,)),
                dma((ys,)), dma((ys,)),
                dma((rows,)), dma((rows,)), dma((rows,)), dma((rows,)),
            ],
            compiler_params=pltpu.CompilerParams(
                collective_id=0, has_side_effects=True, vmem_limit_bytes=60 * 2**20
            ),
        )(slots, pool, panel, prev, pivot.reshape(rows, slab, wide), top, diag)
        return column[None], cross[None], new_diag.reshape(1, width, wide)

    in_specs = (
        P("prow", "pcol"),
        P(None, "prow", None),
        P(None, "prow", None),
        P(None, "pcol", None),
        P("pcol", "prow"),
        P("pcol", None),
        P(),
    )
    out_specs = (P(None, "pcol", "prow"), P(None, "pcol", None), P(None, "pcol", None))
    return jax.shard_map(body, mesh=mesh, in_specs=in_specs, out_specs=out_specs, check_vma=False)
```
